256 devices in a mesh: occ: 32 (over x, z), vir: 8 (over y, core).
Axes of the slice: x: 4, y: 4, z: 8, core: 2. Of those that a mesh axis runs over, the one named last changes fastest.
Arguments:
- t2_amps: float32 [16384, 4096], P('occ', 'vir'), may hold values from -0.046875 to 0.046875
- lambda_amps: float32 [16384, 4096], P('occ', 'vir'), may hold values from -6 to 6
- live_pairs: int32 [32], P('occ'), may hold values from 64 to 512, as said below
- block_sizes: int32 [8], replicated, may hold values from 64 to 2560, as said below
Outputs:
- density: float32 [4096, 4096], P('occ', 'vir')
The draws below stay inside these ranges and needn't reach their ends.
Inputs may be any that keep to these rules, and one draw needn't show every extreme that they name: Slots 0 to live_pairs[k] - 1 of block k are live; some block has all 512 live. `block_sizes`: the blocks tile the 4096 columns in order and sum to 4096; some block has exactly 64 columns and some exactly 2560.
All inputs are finite; a program needn't handle non-finite values.
Results may differ from the reference program's by a relative error of at most 0.00015.
Values sent between devices are 32-bit elements; how exact they have to be, the bound alone decides.
No kernel may reach another device: no remote copies, remote signals or barrier semaphores. Data moves between devices by JAX's collectives and lax.ppermute only.
A program may use at most 128 MiB of HBM per device.

```python
import jax
import jax.numpy as jnp
from jax import lax

P_DEV = 512
OCC_DEVS = 32
PAIRS = 16384
V = 4096
BLK_MIN = 64
BLK_MAX = 2560


def draw_live_pairs(key, part):
    key = jax.random.fold_in(key, 9)
    first, second = jax.random.split(key)
    spread = jax.random.randint(first, (OCC_DEVS,), 0, P_DEV)
    counts = jnp.maximum(P_DEV // 8, spread * spread // P_DEV)
    chosen = jax.random.randint(second, (), 0, OCC_DEVS)
    return counts.at[chosen].set(P_DEV).astype(jnp.int32)


def draw_block_sizes(key, part):
    key = jax.random.fold_in(key, 5)
    first, second = jax.random.split(key)
    limit = BLK_MAX - BLK_MIN
    extra = V - BLK_MAX - 7 * BLK_MIN
    base = extra // 6
    remain = extra - 6 * base
    spread_max = max(0, min(base, limit - base - 1))
    deltas = jax.random.randint(first, (3,), -spread_max, spread_max + 1)
    signed = jnp.stack([deltas[0], -deltas[0], deltas[1], -deltas[1], deltas[2], -deltas[2]])
    bumps = (jnp.arange(6, dtype=jnp.int32) < remain).astype(jnp.int32)
    middle = BLK_MIN + base + bumps + signed
    sizes = jnp.concatenate([jnp.array([BLK_MIN, BLK_MAX], jnp.int32), middle.astype(jnp.int32)])
    order = jax.random.permutation(second, 8)
    return sizes[order].astype(jnp.int32)


def raised(values, rng, source, target, shards_of, factor):
    def block_of(position):
        return (jnp.arange(values.shape[position]) // (values.shape[position] // shards_of)).reshape((-1,) + (1,) * (values.ndim - 1 - position))

    one_side = jax.random.permutation(rng, shards_of)[block_of(target)]
    far = (block_of(target) + shards_of // 2) % shards_of
    return jnp.where((block_of(source) == one_side) | (block_of(source) == far), factor * values, values)


def steps_of(rng, dims, pieces, least, top_value):
    level, own = 1.0, jax.random.fold_in(rng, 6)
    for position, shards_of in pieces:
        draws = jnp.exp(jax.random.uniform(jax.random.fold_in(own, position), (shards_of,), jnp.float32, least / len(pieces), top_value / len(pieces)))
        level = level * jnp.repeat(draws, dims[position] // shards_of).reshape([-1 if axis == position else 1 for axis in range(len(dims))])
    return level


def scatter_about(stream_key, extent, deviation, reach, cuts=(), kind=jnp.bfloat16):
    drawn = jax.random.normal(stream_key, extent, jnp.float32) * deviation
    if len(cuts) > 0:
        drawn = steps_of(stream_key, extent, cuts, -0.22, 0.18) * drawn
    return jnp.clip(drawn, min=-reach, max=reach).astype(kind)


def noise_with(rng, dims, width, reach, pieces, heavy, kind=jnp.bfloat16):
    drawn = width * jax.random.normal(rng, dims, jnp.float32)
    if pieces:
        drawn = drawn * steps_of(rng, dims, pieces, -0.22, 0.18)
    return jnp.clip(raised(drawn, jax.random.fold_in(rng, 3), *heavy), -reach, reach).astype(kind)


def setup_inputs(seed: int = 0) -> dict:
    key_of = jax.random.split(jax.random.key(seed), 5)
    return {
        "t2_amps": scatter_about(key_of[0], (PAIRS, V), PAIRS ** -0.5, 0.046875, ((0, 32), (1, 8)), jnp.float32),
        "lambda_amps": noise_with(key_of[1], (PAIRS, V), 1.0, 6.0, ((0, 32), (1, 8)), (0, 1, 32, 2.75), jnp.float32),
        "live_pairs": draw_live_pairs(jax.random.fold_in(key_of[4], 71), 0),
        "block_sizes": draw_block_sizes(jax.random.fold_in(key_of[4], 71), 0),
    }


def irrep_labels(index, sizes):
    ends = jnp.cumsum(sizes)
    return jnp.sum((index[:, None] >= ends[None, :]).astype(jnp.int32), axis=1)


def reference(t2_amps, lambda_amps, live_pairs, block_sizes):
    slots = jnp.arange(PAIRS, dtype=jnp.int32)
    owner = slots // P_DEV
    within = slots % P_DEV
    live = (within < live_pairs[owner]).astype(jnp.float32)
    weighted = lambda_amps * live[:, None]
    summed = lax.dot_general(weighted, t2_amps, (((0,), (0,)), ((), ())), precision=lax.Precision.HIGHEST, preferred_element_type=jnp.float32)
    labels = irrep_labels(jnp.arange(V, dtype=jnp.int32), block_sizes)
    same = (labels[:, None] == labels[None, :]).astype(jnp.float32)
    return summed * same
```

```python
import functools
import jax
import jax.numpy as jnp
from jax import lax
from jax.experimental import pallas as pl
from jax.experimental.pallas import tpu as pltpu
from jax.sharding import Mesh, PartitionSpec as P

NX, NZ, NY, NC = 4, 8, 4, 2
V = 4096
K = 512
W = 512
SUB = 64
STREAMS = (("A", 32), ("A", 32))
ZORDER = (4, 3, -3, 2, -2, 1, -1, 0)


def ring(n, step):
    return [(i, (i + step) % n) for i in range(n)]


def shift(value, axis, n, step):
    return lax.ppermute(value, axis, ring(n, step))


def chunk_kernel(kind, rows, sub, scalars, b0, b1, b2, b3, thi, tlo, lims, out, stage):
    x, z, y, c = scalars[0], scalars[1], scalars[2], scalars[3]
    zz = scalars[4 + pl.program_id(0)]
    lam = jnp.concatenate([b0[0], b1[0], b2[0], b3[0]], axis=0)
    hi = lam.astype(jnp.bfloat16)
    lo = (lam - hi.astype(jnp.float32)).astype(jnp.bfloat16)
    dot = functools.partial(jnp.dot, preferred_element_type=jnp.float32)
    acc = dot(hi, thi[...]) + (dot(lo, thi[...]) + dot(hi, tlo[...]))
    first = lims[0:1, :]
    last = lims[1:2, :]
    place = lax.broadcasted_iota(jnp.int32, (rows, 1), 0)
    for rel in range(NY):
        xp = lax.rem(y + rel, NY)
        row = place + (xp * 1024 + zz * 128 + c * SUB + sub)
        part = acc[rel * rows:(rel + 1) * rows]
        part = jnp.where((row >= first) & (row < last), part, 0.0)
        if kind == "A":
            stage[xp] = part
        else:
            away = lax.rem(xp - x + NX, NX)
            spot = jnp.where(away == 2, 0, jnp.where(away == 0, 3, jnp.where(away == 1, 1, 2)))
            out[spot, 0] = part
    if kind == "A":
        out[0, 0] = stage[0] + stage[3]
        out[0, 1] = stage[1]
        out[0, 2] = stage[2]


def chunks(kind, rows, sub, scalars, blocks, thi, tlo, lims):
    lam_spec = pl.BlockSpec((1, rows, K), lambda k, s: (s[4 + k], 0, 0))
    whole = lambda shape: pl.BlockSpec(shape, lambda k, s: (0, 0))
    if kind == "A":
        shape, block = (NZ, 3, rows, 2 * W), (1, 3, rows, 2 * W)
        out_map = lambda k, s: (k, 0, 0, 0)
    else:
        shape, block = (NX, NZ, rows, 2 * W), (NX, 1, rows, 2 * W)
        out_map = lambda k, s: (0, k, 0, 0)
    return pl.pallas_call(
        functools.partial(chunk_kernel, kind, rows, sub),
        out_shape=jax.ShapeDtypeStruct(shape, jnp.float32),
        grid_spec=pltpu.PrefetchScalarGridSpec(
            num_scalar_prefetch=1,
            grid=(NZ,),
            in_specs=[lam_spec] * 4 + [whole((K, 2 * W))] * 2 + [whole((2, 2 * W))],
            out_specs=pl.BlockSpec(block, out_map),
            scratch_shapes=[pltpu.VMEM((NX, rows, 2 * W), jnp.float32)],
        ),
        compiler_params=pltpu.CompilerParams(vmem_limit_bytes=24 * 1024 * 1024),
        cost_estimate=pl.CostEstimate(
            flops=2 * 3 * NZ * 4 * rows * K * 2 * W,
            bytes_accessed=NZ * 4 * rows * K * 4 + 4 * K * 2 * W + NZ * 4 * rows * 2 * W * 4,
            transcendentals=0,
        ),
    )(scalars, *blocks, thi, tlo, lims)


def add_left(full, left):
    n = left.shape[-1]
    return jnp.concatenate([full[..., :n] + left, full[..., n:]], axis=-1)


def add_right(full, right):
    n = full.shape[-1] - right.shape[-1]
    return jnp.concatenate([full[..., :n], full[..., n:] + right], axis=-1)


def z_phase(part):
    half = part.shape[-1] // 2
    up = shift(part[0][..., :half], "z", NZ, 1)
    down = shift(part[0][..., half:], "z", NZ, -1)
    up = shift(add_left(part[1], up), "z", NZ, 1)
    down = shift(add_right(part[2], down), "z", NZ, -1)
    up = shift(part[3] + up, "z", NZ, 1)
    down = shift(part[4] + down, "z", NZ, -1)
    up = shift(part[5] + up, "z", NZ, 1)
    down = shift(part[6] + down, "z", NZ, -1)
    return part[7] + up + down


def stream_a(part, x):
    got = z_phase(part)
    slot = lambda d: lax.dynamic_index_in_dim(got, lax.rem(lax.rem(x + d, NX), 3), 0, keepdims=False)
    right = shift(slot(1), "x", NX, 1)
    left = shift(slot(3), "x", NX, 3)
    far = shift(slot(2), "x", NX, 2)
    return slot(0) + right + left + far


def stream_b(part):
    half = part.shape[-1] // 2
    up = shift(part[0][..., :half], "x", NX, 1)
    down = shift(part[0][..., half:], "x", NX, -1)
    up = shift(add_left(part[1], up), "x", NX, 1)
    down = shift(add_right(part[2], down), "x", NX, -1)
    return z_phase(part[3] + up + down)


def body(t2_amps, lambda_amps, live_pairs, block_sizes):
    x, z, y, c = (lax.axis_index(name).astype(jnp.int32) for name in "xzyc")
    swap = ring(NC, 1)
    order = [lax.rem(z + (d + NZ), NZ) for d in ZORDER]
    scalars = jnp.stack([x, z, y, c] + order).astype(jnp.int32)

    ends = jnp.cumsum(block_sizes)
    starts = ends - block_sizes
    cols = (y * 2 * W + jnp.arange(2 * W, dtype=jnp.int32))[None, :]
    inside = (cols >= starts[:, None]) & (cols < ends[:, None])
    lims = jnp.stack([
        jnp.sum(jnp.where(inside, starts[:, None], 0), axis=0),
        jnp.sum(jnp.where(inside, ends[:, None], 0), axis=0),
    ]).astype(jnp.int32)

    lam_rows = lambda_amps.T.reshape(4, NC, SUB, K)
    keep = lax.dynamic_index_in_dim(lam_rows, c, 1, keepdims=False)
    give = lax.dynamic_index_in_dim(lam_rows, 1 - c, 1, keepdims=False)
    both = lambda mine, other, axis: jnp.where(
        c == 0, jnp.concatenate([mine, other], axis), jnp.concatenate([other, mine], axis)
    )

    blocks = []
    sub = 0
    for kind, rows in STREAMS:
        mine = keep[:, sub:sub + rows]
        other = lax.ppermute(give[:, sub:sub + rows], "c", swap)
        own = both(mine, other, 0)
        blocks.append((
            own,
            shift(own, "y", NY, -1),
            shift(own, "y", NY, 2),
            shift(own, "y", NY, 1),
        ))
        sub += rows

    t2_pair = both(t2_amps, lax.ppermute(t2_amps, "c", swap), 1)
    live = jnp.arange(K, dtype=jnp.int32)[:, None] < live_pairs[0]
    t2_pair = jnp.where(live, t2_pair, 0.0)
    t2_top = lax.reduce_precision(t2_pair, 8, 7)
    thi = t2_top.astype(jnp.bfloat16)
    tlo = (t2_pair - t2_top).astype(jnp.bfloat16)

    done = []
    sub = 0
    for (kind, rows), block in zip(STREAMS, blocks):
        part = chunks(kind, rows, sub, scalars, block, thi, tlo, lims)
        got = stream_a(part, x) if kind == "A" else stream_b(part)
        row = (x * 1024 + z * 128 + c * SUB + sub + jnp.arange(rows, dtype=jnp.int32))[:, None]
        done.append(jnp.where((row >= lims[0:1]) & (row < lims[1:2]), got, 0.0))
        sub += rows

    rows_all = jnp.concatenate(done, axis=0).reshape(SUB, NC, W)
    mine = lax.dynamic_index_in_dim(rows_all, c, 1, keepdims=False)
    other = lax.ppermute(lax.dynamic_index_in_dim(rows_all, 1 - c, 1, keepdims=False), "c", swap)
    return both(mine, other, 0)


def solution(mesh):
    fine = Mesh(mesh.devices.reshape(NX, NZ, NY, NC), ("x", "z", "y", "c"))
    spec = P(("x", "z"), ("y", "c"))
    return jax.shard_map(
        body,
        mesh=fine,
        in_specs=(spec, spec, P(("x", "z")), P()),
        out_specs=spec,
        check_vma=False,
    )
```

```python
import functools
import jax
import jax.numpy as jnp
from jax import lax
from jax.experimental import pallas as pl
from jax.experimental.pallas import tpu as pltpu
from jax.sharding import Mesh, PartitionSpec as P

NX, NZ, NY, NC = 4, 8, 4, 2
V = 4096
K = 512
W = 512
SUB = 64
STREAMS = (("A", 32), ("A", 32))
ZORDER = (4, 3, -3, 2, -2, 1, -1, 0)


def ring(n, step):
    return [(i, (i + step) % n) for i in range(n)]


def shift(value, axis, n, step):
    return lax.ppermute(value, axis, ring(n, step))


def chunk_kernel(kind, rows, sub, first_k, scalars, b0, b1, b2u, b2d, b3, thi, tlo, lims, out, stage):
    x, z, y, c = scalars[0], scalars[1], scalars[2], scalars[3]
    zz = scalars[4 + first_k + pl.program_id(0)]
    lam = jnp.concatenate([b0[zz], b1[zz], b2u[zz], b2d[zz], b3[zz]], axis=0)
    hi = lam.astype(jnp.bfloat16)
    lo = (lam - hi.astype(jnp.float32)).astype(jnp.bfloat16)
    dot = functools.partial(jnp.dot, preferred_element_type=jnp.float32)
    acc = dot(hi, thi[...]) + (dot(lo, thi[...]) + dot(hi, tlo[...]))
    first = lims[0:1, :]
    last = lims[1:2, :]
    place = lax.broadcasted_iota(jnp.int32, (rows, 1), 0)
    for rel in range(NY):
        xp = lax.rem(y + rel, NY)
        row = place + (xp * 1024 + zz * 128 + c * SUB + sub)
        part = acc[rel * rows:(rel + 1) * rows]
        part = jnp.where((row >= first) & (row < last), part, 0.0)
        if kind == "A":
            stage[xp] = part
        else:
            away = lax.rem(xp - x + NX, NX)
            spot = jnp.where(away == 2, 0, jnp.where(away == 0, 3, jnp.where(away == 1, 1, 2)))
            out[spot, 0] = part
    if kind == "A":
        out[0, 0] = stage[0] + stage[3]
        out[0, 1] = stage[1]
        out[0, 2] = stage[2]


def chunks(kind, rows, sub, scalars, blocks, thi, tlo, lims, first_k=0, count=NZ):
    whole = pl.BlockSpec(memory_space=pltpu.VMEM)
    if kind == "A":
        shape, block = (count, 3, rows, 2 * W), (1, 3, rows, 2 * W)
        out_map = lambda k, s: (k, 0, 0, 0)
    else:
        shape, block = (NX, count, rows, 2 * W), (NX, 1, rows, 2 * W)
        out_map = lambda k, s: (0, k, 0, 0)
    return pl.pallas_call(
        functools.partial(chunk_kernel, kind, rows, sub, first_k),
        out_shape=jax.ShapeDtypeStruct(shape, jnp.float32),
        grid_spec=pltpu.PrefetchScalarGridSpec(
            num_scalar_prefetch=1,
            grid=(count,),
            in_specs=[whole] * 8,
            out_specs=pl.BlockSpec(block, out_map),
            scratch_shapes=[pltpu.VMEM((NX, rows, 2 * W), jnp.float32)],
        ),
        compiler_params=pltpu.CompilerParams(vmem_limit_bytes=24 * 1024 * 1024),
        cost_estimate=pl.CostEstimate(
            flops=2 * 3 * count * 4 * rows * K * 2 * W,
            bytes_accessed=count * 4 * rows * K * 4 + 4 * K * 2 * W + count * 4 * rows * 2 * W * 4,
            transcendentals=0,
        ),
    )(scalars, *blocks, thi, tlo, lims)


def add_left(full, left):
    n = left.shape[-1]
    return jnp.concatenate([full[..., :n] + left, full[..., n:]], axis=-1)


def add_right(full, right):
    n = full.shape[-1] - right.shape[-1]
    return jnp.concatenate([full[..., :n], full[..., n:] + right], axis=-1)


def z_phase(part):
    half = part[0].shape[-1] // 2
    both = lax.optimization_barrier
    up = shift(part[0][..., :half], "z", NZ, 1)
    down = shift(part[0][..., half:], "z", NZ, -1)
    up, down = both((up, down))
    up, down = both((add_left(part[1], up), add_right(part[2], down)))
    up, down = shift(up, "z", NZ, 1), shift(down, "z", NZ, -1)
    for k in (3, 5):
        up, down = both((up, down))
        up, down = both((part[k] + up, part[k + 1] + down))
        up, down = shift(up, "z", NZ, 1), shift(down, "z", NZ, -1)
    return part[7] + up + down


def stream_a(part, x):
    got = z_phase(part)
    slot = lambda d: lax.dynamic_index_in_dim(got, lax.rem(lax.rem(x + d, NX), 3), 0, keepdims=False)
    right = shift(slot(1), "x", NX, 1)
    left = shift(slot(3), "x", NX, 3)
    far = shift(slot(2), "x", NX, 2)
    return slot(0) + right + left + far


def stream_b(part):
    half = part[0].shape[-1] // 2
    up = shift(part[0][..., :half], "x", NX, 1)
    down = shift(part[0][..., half:], "x", NX, -1)
    up = shift(add_left(part[1], up), "x", NX, 1)
    down = shift(add_right(part[2], down), "x", NX, -1)
    return z_phase(part[3] + up + down)


def body(t2_amps, lambda_amps, live_pairs, block_sizes):
    x, z, y, c = (lax.axis_index(name).astype(jnp.int32) for name in "xzyc")
    swap = ring(NC, 1)
    order = [lax.rem(z + (d + NZ), NZ) for d in ZORDER]
    scalars = jnp.stack([x, z, y, c] + order).astype(jnp.int32)

    ends = jnp.cumsum(block_sizes)
    starts = ends - block_sizes
    cols = (y * 2 * W + jnp.arange(2 * W, dtype=jnp.int32))[None, :]
    inside = (cols >= starts[:, None]) & (cols < ends[:, None])
    lims = jnp.stack([
        jnp.sum(jnp.where(inside, starts[:, None], 0), axis=0),
        jnp.sum(jnp.where(inside, ends[:, None], 0), axis=0),
    ]).astype(jnp.int32)

    lam_rows = lambda_amps.T.reshape(4, NC, SUB, K)
    keep = lax.dynamic_index_in_dim(lam_rows, c, 1, keepdims=False)
    give = lax.dynamic_index_in_dim(lam_rows, 1 - c, 1, keepdims=False)
    both = lambda mine, other, axis: jnp.where(
        c == 0, jnp.concatenate([mine, other], axis), jnp.concatenate([other, mine], axis)
    )

    barrier = lax.optimization_barrier
    t2_other = lax.ppermute(t2_amps, "c", swap)
    live = jnp.arange(K, dtype=jnp.int32)[:, None] < live_pairs[0]
    blocks = []
    sub = 0
    for kind, rows in STREAMS:
        mine = keep[:, sub:sub + rows]
        other = lax.ppermute(give[:, sub:sub + rows], "c", swap)
        own = both(mine, other, 0)
        if blocks:
            own, thi = barrier((own, thi))
        up = shift(own, "y", NY, 1)
        down = shift(own, "y", NY, -1)
        if not blocks:
            up, down, t2_other = barrier((up, down, t2_other))
            t2_pair = jnp.where(live, both(t2_amps, t2_other, 1), 0.0)
            t2_top = lax.reduce_precision(t2_pair, 8, 7)
            thi = t2_top.astype(jnp.bfloat16)
            tlo = (t2_pair - t2_top).astype(jnp.bfloat16)
        far_up = shift(up[:, :rows // 2], "y", NY, 1)
        far_down = shift(down[:, rows // 2:], "y", NY, -1)
        blocks.append((own, down, far_up, far_down, up))
        sub += rows

    done = []
    sub = 0
    for (kind, rows), block in zip(STREAMS, blocks):
        if kind == "A":
            head = chunks(kind, rows, sub, scalars, block, thi, tlo, lims, 0, 3)
            tail = chunks(kind, rows, sub, scalars, block, thi, tlo, lims, 3, 5)
            part = [head[k] for k in range(3)] + [tail[k] for k in range(5)]
        else:
            part = chunks(kind, rows, sub, scalars, block, thi, tlo, lims)
        got = stream_a(part, x) if kind == "A" else stream_b(part)
        row = (x * 1024 + z * 128 + c * SUB + sub + jnp.arange(rows, dtype=jnp.int32))[:, None]
        done.append(jnp.where((row >= lims[0:1]) & (row < lims[1:2]), got, 0.0))
        sub += rows

    rows_all = jnp.concatenate(done, axis=0).reshape(SUB, NC, W)
    mine = lax.dynamic_index_in_dim(rows_all, c, 1, keepdims=False)
    other = lax.ppermute(lax.dynamic_index_in_dim(rows_all, 1 - c, 1, keepdims=False), "c", swap)
    return both(mine, other, 0)


def solution(mesh):
    fine = Mesh(mesh.devices.reshape(NX, NZ, NY, NC), ("x", "z", "y", "c"))
    spec = P(("x", "z"), ("y", "c"))
    return jax.shard_map(
        body,
        mesh=fine,
        in_specs=(spec, spec, P(("x", "z")), P()),
        out_specs=spec,
        check_vma=False,
    )
```

```python
import functools
import jax
import jax.numpy as jnp
from jax import lax
from jax.experimental import pallas as pl
from jax.experimental.pallas import tpu as pltpu
from jax.sharding import Mesh, PartitionSpec as P

NX, NZ, NY, NC = 4, 8, 4, 2
K = 512
W = 512
SUB = 64
PART = 32
ZORDER = (4, 3, -3, 2, -2, 1, -1, 0)
HEAD = 3
GROUPS = 8


def even(n):
    return [(i, i ^ 1) for i in range(n)]


def odd(n):
    return [(i, (i + 1) % n if i % 2 else (i - 1) % n) for i in range(n)]


def flip(n, bits):
    return [(i, i ^ bits) for i in range(n)]


tie = lax.optimization_barrier


def place_of():
    return tuple(lax.axis_index(name).astype(jnp.int32) for name in "xzyc")


def chunk_kernel(first_k, count, adds, sizes, b0, b1, b2u, b2d, b3, top, low, *refs):
    before, outs, stage = refs[:adds], refs[adds:-1], refs[-1]
    x, z, y, c = place_of()
    sign = 1 - 2 * (z & 1)
    order = [(z + d * sign) & (NZ - 1) for d in ZORDER[first_k:first_k + count]]
    lam = []
    for zz in order:
        lam += [b0[zz], b1[zz], b2u[zz], b2d[zz], b3[zz]]
    lam = jnp.concatenate(lam, axis=0)
    hi = lam.astype(jnp.bfloat16)
    lo = (lam - hi.astype(jnp.float32)).astype(jnp.bfloat16)
    dot = functools.partial(jnp.dot, preferred_element_type=jnp.float32)
    acc = dot(hi, top[...]) + (dot(lo, top[...]) + dot(hi, low[...]))
    cols = y * 2 * W + lax.broadcasted_iota(jnp.int32, (1, 2 * W), 1)
    first = jnp.zeros((1, 2 * W), jnp.int32)
    last = first
    begin = jnp.int32(0)
    for g in range(GROUPS):
        end = begin + sizes[g]
        inside = (cols >= begin) & (cols < end)
        first = jnp.where(inside, begin, first)
        last = jnp.where(inside, end, last)
        begin = end
    place = c * SUB + (x & 1) * PART + lax.broadcasted_iota(jnp.int32, (PART, 1), 0)
    for k, zz in enumerate(order):
        for rel in range(NY):
            xp = y ^ rel
            row = place + (xp * 1024 + zz * 128)
            at = (k * NY + rel) * PART
            stage[xp] = jnp.where((row >= first) & (row < last), acc[at:at + PART], 0.0)
        for slot in range(3):
            value = stage[0] + stage[3] if slot == 0 else stage[slot]
            for h in range(2):
                piece = value[:, h * W:(h + 1) * W]
                if adds:
                    piece = piece + before[h][first_k + k, slot]
                outs[h][k, slot] = piece


def chunks(sizes, blocks, t2_parts, before, first_k, count):
    whole = pl.BlockSpec(memory_space=pltpu.VMEM)
    return pl.pallas_call(
        functools.partial(chunk_kernel, first_k, count, len(before)),
        out_shape=[jax.ShapeDtypeStruct((count, 3, PART, W), jnp.float32)] * 2,
        in_specs=[pl.BlockSpec(memory_space=pltpu.SMEM)] + [whole] * (7 + len(before)),
        out_specs=[whole, whole],
        scratch_shapes=[pltpu.VMEM((NX, PART, 2 * W), jnp.float32)],
        compiler_params=pltpu.CompilerParams(vmem_limit_bytes=20 * 1024 * 1024),
        cost_estimate=pl.CostEstimate(
            flops=2 * 3 * count * 4 * PART * K * 2 * W,
            bytes_accessed=count * 4 * PART * K * 4 + 4 * K * 2 * W + count * 3 * PART * 2 * W * 4,
            transcendentals=0,
        ),
    )(sizes, *blocks, *t2_parts, *before)


def add_left(full, left):
    n = left.shape[-1]
    return jnp.concatenate([full[..., :n] + left, full[..., n:]], axis=-1)


def add_right(full, right):
    n = full.shape[-1] - right.shape[-1]
    return jnp.concatenate([full[..., :n], full[..., n:] + right], axis=-1)


def step(value, other, axis, n):
    return lax.ppermute(value, axis, even(n)), lax.ppermute(other, axis, odd(n))


def z_phase(part):
    half = part[0].shape[-1] // 2
    one, two = step(part[0][..., :half], part[0][..., half:], "z", NZ)
    one, two = tie((one, two))
    one, two = step(*tie((add_right(part[1], two), add_left(part[2], one))), "z", NZ)
    for k in (3, 5):
        one, two = tie((one, two))
        one, two = step(*tie((part[k] + two, part[k + 1] + one)), "z", NZ)
    return part[7] + one + two


def split_kernel(masked, count, mine, other, top, low):
    live = lax.broadcasted_iota(jnp.int32, (K, 1), 0) < (count[0] if masked else K)
    c = lax.axis_index("c")

    def put(ref, at):
        value = jnp.where(live, ref[...], 0.0)
        hi = value.astype(jnp.bfloat16)
        top[:, at:at + W] = hi
        low[:, at:at + W] = (value - hi.astype(jnp.float32)).astype(jnp.bfloat16)

    @pl.when(c == 0)
    def _():
        put(mine, 0)
        put(other, W)

    @pl.when(c != 0)
    def _():
        put(other, 0)
        put(mine, W)


def split(masked, count, mine, other):
    whole = pl.BlockSpec(memory_space=pltpu.VMEM)
    return pl.pallas_call(
        functools.partial(split_kernel, masked),
        out_shape=[jax.ShapeDtypeStruct((K, 2 * W), jnp.bfloat16)] * 2,
        in_specs=[pl.BlockSpec(memory_space=pltpu.SMEM), whole, whole],
        out_specs=[whole, whole],
        compiler_params=pltpu.CompilerParams(vmem_limit_bytes=8 * 1024 * 1024),
        cost_estimate=pl.CostEstimate(flops=0, bytes_accessed=16 * K * W, transcendentals=0),
    )(count, mine, other)


def finish_kernel(sizes, mine, other, out):
    x, z, y, c = place_of()
    col = y * 2 * W + c * W + lax.broadcasted_iota(jnp.int32, (1, W), 1)
    first = jnp.zeros((1, W), jnp.int32)
    last = first
    begin = jnp.int32(0)
    for g in range(GROUPS):
        end = begin + sizes[g]
        inside = (col >= begin) & (col < end)
        first = jnp.where(inside, begin, first)
        last = jnp.where(inside, end, last)
        begin = end

    def put(ref, at):
        row = x * 1024 + z * 128 + at + lax.broadcasted_iota(jnp.int32, (SUB, 1), 0)
        out[at:at + SUB] = jnp.where((row >= first) & (row < last), ref[...], 0.0)

    @pl.when(c == 0)
    def _():
        put(mine, 0)
        put(other, SUB)

    @pl.when(c != 0)
    def _():
        put(other, 0)
        put(mine, SUB)


def finish(sizes, mine, other):
    whole = pl.BlockSpec(memory_space=pltpu.VMEM)
    return pl.pallas_call(
        finish_kernel,
        out_shape=jax.ShapeDtypeStruct((2 * SUB, W), jnp.float32),
        in_specs=[pl.BlockSpec(memory_space=pltpu.SMEM), whole, whole],
        out_specs=whole,
        compiler_params=pltpu.CompilerParams(vmem_limit_bytes=4 * 1024 * 1024),
        cost_estimate=pl.CostEstimate(flops=0, bytes_accessed=16 * SUB * W, transcendentals=0),
    )(sizes, mine, other)


def body(t2_amps, lambda_amps, live_pairs, block_sizes):
    x, c = (lax.axis_index(name).astype(jnp.int32) for name in "xc")
    swap = flip(NC, 1)
    places = [c, 1 - c, x & 1, 1 - (x & 1)] + [lax.rem(x ^ d, 3) for d in range(NX)]
    places = [place.astype(jnp.uint32) for place in places]
    lambda_amps, places, low_c, low_p = tie((lambda_amps, places, c == 0, (x & 1) == 0))
    c, not_c, p, not_p, *slots = places
    pick = lambda a, i, axis: lax.dynamic_index_in_dim(a, i, axis, keepdims=False, allow_negative_indices=False)

    def both(at, mine, other, axis):
        return jnp.where(at, jnp.concatenate([mine, other], axis), jnp.concatenate([other, mine], axis))

    lam_rows = lambda_amps.T.reshape(4, NC, SUB, K)
    keep, give = pick(lam_rows, c, 1), pick(lam_rows, not_c, 1)
    live = jnp.arange(K, dtype=jnp.int32)[:, None] < live_pairs[0]
    near = both(low_c, keep, lax.ppermute(give, "c", swap), 0).reshape(NZ, 2, PART, K)
    own = pick(near, p, 1)
    one, two = step(own, own, "y", NY)
    pair = lax.ppermute(pick(near, not_p, 1), "x", flip(NX, 1))

    t2_send, _ = tie((t2_amps, pair))
    t2_par = lax.ppermute(jnp.where(live, t2_send, 0.0), "x", flip(NX, 1))
    t2_own = split(True, live_pairs, t2_amps, lax.ppermute(t2_amps, "c", swap))

    half = PART // 2
    fars = two[:, half:], one[:, :half]
    pair, _ = tie((pair, (fars, t2_own)))
    far_down, far_up = step(*fars, "y", NY)
    blocks = (own, one, far_up, far_down, two)
    one, two = step(pair, pair, "y", NY)
    first = chunks(block_sizes, blocks, t2_own, (), 0, NZ)

    fars = two[:, half:], one[:, :half]
    fars, _ = tie((fars, (far_down, far_up)))
    t2_par, _ = tie((t2_par, fars))
    t2_both, _ = tie(((t2_par, lax.ppermute(t2_par, "c", swap)), first))
    t2_par = split(False, live_pairs, *t2_both)
    far_down, far_up = step(*fars, "y", NY)
    blocks = (pair, one, far_up, far_down, two)
    head = chunks(block_sizes, blocks, t2_par, first, 0, HEAD)
    tail = chunks(block_sizes, blocks, t2_par, first, HEAD, NZ - HEAD)

    done = []
    for h in range(2):
        got = z_phase([head[h][k] for k in range(HEAD)] + [tail[h][k] for k in range(NZ - HEAD)])
        slot = lambda d: pick(got, slots[d], 0)
        far = lax.ppermute(slot(2), "x", flip(NX, 2))
        near = lax.ppermute(slot(1), "x", flip(NX, 1))
        wrap = lax.ppermute(slot(3), "x", flip(NX, 3))
        done.append(both(low_p, slot(0) + far, near + wrap, 0))

    mine = jnp.where(low_c, done[0], done[1])
    other = lax.ppermute(jnp.where(low_c, done[1], done[0]), "c", swap)
    return finish(block_sizes, mine, other)


def solution(mesh):
    fine = Mesh(mesh.devices.reshape(NX, NZ, NY, NC), ("x", "z", "y", "c"))
    spec = P(("x", "z"), ("y", "c"))
    return jax.shard_map(
        body,
        mesh=fine,
        in_specs=(spec, spec, P(("x", "z")), P()),
        out_specs=spec,
        check_vma=False,
    )
```

```python
import functools
import jax
import jax.numpy as jnp
from jax import lax
from jax.experimental import pallas as pl
from jax.experimental.pallas import tpu as pltpu
from jax.sharding import Mesh, PartitionSpec as P

NX, NZ, NY, NC = 4, 8, 4, 2
K = 512
W = 512
SUB = 64
PART = 32
ZORDER = (4, 3, -3, 2, -2, 1, -1, 0)
HEAD = 3
GROUPS = 8


def even(n):
    return [(i, i ^ 1) for i in range(n)]


def odd(n):
    return [(i, (i + 1) % n if i % 2 else (i - 1) % n) for i in range(n)]


def flip(n, bits):
    return [(i, i ^ bits) for i in range(n)]


tie = lax.optimization_barrier


def place_of():
    return tuple(lax.axis_index(name).astype(jnp.int32) for name in "xzyc")


def chunk_kernel(first_k, count, adds, sizes, b0, b1, b2u, b2d, b3, top, low, *refs):
    before, outs, stage = refs[:adds], refs[adds:-1], refs[-1]
    x, z, y, c = place_of()
    sign = 1 - 2 * (z & 1)
    order = [(z + d * sign) & (NZ - 1) for d in ZORDER[first_k:first_k + count]]
    lam = []
    for zz in order:
        lam += [b0[zz], b1[zz], b2u[zz], b2d[zz], b3[zz]]
    lam = jnp.concatenate(lam, axis=0)
    hi = lam.astype(jnp.bfloat16)
    lo = (lam - hi.astype(jnp.float32)).astype(jnp.bfloat16)
    dot = functools.partial(jnp.dot, preferred_element_type=jnp.float32)
    acc = dot(hi, top[...]) + (dot(lo, top[...]) + dot(hi, low[...]))
    cols = y * 2 * W + lax.broadcasted_iota(jnp.int32, (1, 2 * W), 1)
    first = jnp.zeros((1, 2 * W), jnp.int32)
    last = first
    begin = jnp.int32(0)
    for g in range(GROUPS):
        end = begin + sizes[g]
        inside = (cols >= begin) & (cols < end)
        first = jnp.where(inside, begin, first)
        last = jnp.where(inside, end, last)
        begin = end
    place = c * SUB + (x & 1) * PART + lax.broadcasted_iota(jnp.int32, (PART, 1), 0)
    for k, zz in enumerate(order):
        for rel in range(NY):
            xp = y ^ rel
            row = place + (xp * 1024 + zz * 128)
            at = (k * NY + rel) * PART
            stage[xp] = jnp.where((row >= first) & (row < last), acc[at:at + PART], 0.0)
        for slot in range(3):
            value = stage[0] + stage[3] if slot == 0 else stage[slot]
            for h in range(2):
                piece = value[:, h * W:(h + 1) * W]
                if adds:
                    piece = piece + before[h][first_k + k, slot]
                outs[h][k, slot] = piece


def chunks(sizes, blocks, t2_parts, before, first_k, count):
    whole = pl.BlockSpec(memory_space=pltpu.VMEM)
    return pl.pallas_call(
        functools.partial(chunk_kernel, first_k, count, len(before)),
        out_shape=[jax.ShapeDtypeStruct((count, 3, PART, W), jnp.float32)] * 2,
        in_specs=[pl.BlockSpec(memory_space=pltpu.SMEM)] + [whole] * (7 + len(before)),
        out_specs=[whole, whole],
        scratch_shapes=[pltpu.VMEM((NX, PART, 2 * W), jnp.float32)],
        compiler_params=pltpu.CompilerParams(vmem_limit_bytes=20 * 1024 * 1024),
        cost_estimate=pl.CostEstimate(
            flops=2 * 3 * count * 4 * PART * K * 2 * W,
            bytes_accessed=count * 4 * PART * K * 4 + 4 * K * 2 * W + count * 3 * PART * 2 * W * 4,
            transcendentals=0,
        ),
    )(sizes, *blocks, *t2_parts, *before)


def add_left(full, left):
    n = left.shape[-1]
    return jnp.concatenate([full[..., :n] + left, full[..., n:]], axis=-1)


def add_right(full, right):
    n = full.shape[-1] - right.shape[-1]
    return jnp.concatenate([full[..., :n], full[..., n:] + right], axis=-1)


def step(value, other, axis, n):
    return lax.ppermute(value, axis, even(n)), lax.ppermute(other, axis, odd(n))


def z_first(part):
    half = part[0].shape[-1] // 2
    one, two = tie(step(part[0][..., :half], part[0][..., half:], "z", NZ))
    return tie((add_right(part[1], two), add_left(part[2], one)))


def z_rest(ready, part):
    one, two = step(*ready, "z", NZ)
    for k in (0, 2):
        one, two = tie((one, two))
        one, two = step(*tie((part[k] + two, part[k + 1] + one)), "z", NZ)
    return part[4] + one + two


def split_kernel(masked, count, mine, other, top, low):
    live = lax.broadcasted_iota(jnp.int32, (K, 1), 0) < (count[0] if masked else K)
    c = lax.axis_index("c")

    def put(ref, at):
        value = jnp.where(live, ref[...], 0.0)
        hi = value.astype(jnp.bfloat16)
        top[:, at:at + W] = hi
        low[:, at:at + W] = (value - hi.astype(jnp.float32)).astype(jnp.bfloat16)

    @pl.when(c == 0)
    def _():
        put(mine, 0)
        put(other, W)

    @pl.when(c != 0)
    def _():
        put(other, 0)
        put(mine, W)


def split(masked, count, mine, other):
    whole = pl.BlockSpec(memory_space=pltpu.VMEM)
    return pl.pallas_call(
        functools.partial(split_kernel, masked),
        out_shape=[jax.ShapeDtypeStruct((K, 2 * W), jnp.bfloat16)] * 2,
        in_specs=[pl.BlockSpec(memory_space=pltpu.SMEM), whole, whole],
        out_specs=[whole, whole],
        compiler_params=pltpu.CompilerParams(vmem_limit_bytes=8 * 1024 * 1024),
        cost_estimate=pl.CostEstimate(flops=0, bytes_accessed=16 * K * W, transcendentals=0),
    )(count, mine, other)


def finish_kernel(sizes, mine, other, out):
    x, z, y, c = place_of()
    col = y * 2 * W + c * W + lax.broadcasted_iota(jnp.int32, (1, W), 1)
    first = jnp.zeros((1, W), jnp.int32)
    last = first
    begin = jnp.int32(0)
    for g in range(GROUPS):
        end = begin + sizes[g]
        inside = (col >= begin) & (col < end)
        first = jnp.where(inside, begin, first)
        last = jnp.where(inside, end, last)
        begin = end

    def put(ref, at):
        row = x * 1024 + z * 128 + at + lax.broadcasted_iota(jnp.int32, (SUB, 1), 0)
        out[at:at + SUB] = jnp.where((row >= first) & (row < last), ref[...], 0.0)

    @pl.when(c == 0)
    def _():
        put(mine, 0)
        put(other, SUB)

    @pl.when(c != 0)
    def _():
        put(other, 0)
        put(mine, SUB)


def finish(sizes, mine, other):
    whole = pl.BlockSpec(memory_space=pltpu.VMEM)
    return pl.pallas_call(
        finish_kernel,
        out_shape=jax.ShapeDtypeStruct((2 * SUB, W), jnp.float32),
        in_specs=[pl.BlockSpec(memory_space=pltpu.SMEM), whole, whole],
        out_specs=whole,
        compiler_params=pltpu.CompilerParams(vmem_limit_bytes=4 * 1024 * 1024),
        cost_estimate=pl.CostEstimate(flops=0, bytes_accessed=16 * SUB * W, transcendentals=0),
    )(sizes, mine, other)


def body(t2_amps, lambda_amps, live_pairs, block_sizes):
    x, c = (lax.axis_index(name).astype(jnp.int32) for name in "xc")
    swap = flip(NC, 1)
    places = [c, 1 - c, x & 1, 1 - (x & 1)] + [lax.rem(x ^ d, 3) for d in range(NX)]
    places = [place.astype(jnp.uint32) for place in places]
    lambda_amps, places, low_c, low_p = tie((lambda_amps, places, c == 0, (x & 1) == 0))
    c, not_c, p, not_p, *slots = places
    pick = lambda a, i, axis: lax.dynamic_index_in_dim(a, i, axis, keepdims=False, allow_negative_indices=False)

    def both(at, mine, other, axis):
        return jnp.where(at, jnp.concatenate([mine, other], axis), jnp.concatenate([other, mine], axis))

    lam_rows = lambda_amps.T.reshape(4, NC, SUB, K)
    keep, give = pick(lam_rows, c, 1), pick(lam_rows, not_c, 1)
    live = jnp.arange(K, dtype=jnp.int32)[:, None] < live_pairs[0]
    near = both(low_c, keep, lax.ppermute(give, "c", swap), 0).reshape(NZ, 2, PART, K)
    own = pick(near, p, 1)
    one, two = step(own, own, "y", NY)
    pair = lax.ppermute(pick(near, not_p, 1), "x", flip(NX, 1))

    t2_send, _ = tie((t2_amps, pair))
    t2_par = lax.ppermute(jnp.where(live, t2_send, 0.0), "x", flip(NX, 1))
    t2_own = split(True, live_pairs, t2_amps, lax.ppermute(t2_amps, "c", swap))

    half = PART // 2
    fars = two[:, half:], one[:, :half]
    pair, _ = tie((pair, (fars, t2_own)))
    far_down, far_up = step(*fars, "y", NY)
    blocks = (own, one, far_up, far_down, two)
    one, two = step(pair, pair, "y", NY)
    first = chunks(block_sizes, blocks, t2_own, (), 0, NZ)

    fars = two[:, half:], one[:, :half]
    fars, _ = tie((fars, (far_down, far_up)))
    t2_par, _ = tie((t2_par, fars))
    t2_both, _ = tie(((t2_par, lax.ppermute(t2_par, "c", swap)), first))
    t2_par = split(False, live_pairs, *t2_both)
    far_down, far_up = step(*fars, "y", NY)
    blocks = (pair, one, far_up, far_down, two)
    head = chunks(block_sizes, blocks, t2_par, first, 0, HEAD)
    ready = [z_first(head[h]) for h in range(2)]
    late, ready[0] = tie((block_sizes, ready[0]))
    tail = chunks(late, blocks, t2_par, first, HEAD, NZ - HEAD)
    gots = [z_rest(ready[h], tail[h]) for h in range(2)]
    slot = lambda d: jnp.stack([pick(got, slots[d], 0) for got in gots])
    far = lax.ppermute(slot(2), "x", flip(NX, 2))
    near = lax.ppermute(slot(1), "x", flip(NX, 1))
    wrap = lax.ppermute(slot(3), "x", flip(NX, 3))
    same = slot(0) + far
    (near, wrap), _ = tie(((near, wrap), same))
    done = both(low_p, same, near + wrap, 1)

    mine = jnp.where(low_c, done[0], done[1])
    other = lax.ppermute(jnp.where(low_c, done[1], done[0]), "c", swap)
    return finish(block_sizes, mine, other)


def solution(mesh):
    fine = Mesh(mesh.devices.reshape(NX, NZ, NY, NC), ("x", "z", "y", "c"))
    spec = P(("x", "z"), ("y", "c"))
    return jax.shard_map(
        body,
        mesh=fine,
        in_specs=(spec, spec, P(("x", "z")), P()),
        out_specs=spec,
        check_vma=False,
    )
```

```python
import functools
import jax
import jax.numpy as jnp
from jax import lax
from jax.experimental import pallas as pl
from jax.experimental.pallas import tpu as pltpu
from jax.sharding import Mesh, PartitionSpec as P

NX, NZ, NY, NC = 4, 8, 4, 2
K = 512
W = 512
SUB = 64
PART = 32
ZORDER = (4, 3, -3, 2, -2, 1, -1, 0)
HEAD = 3
EARLY = 64
GROUPS = 8


def even(n):
    return [(i, i ^ 1) for i in range(n)]


def odd(n):
    return [(i, (i + 1) % n if i % 2 else (i - 1) % n) for i in range(n)]


def flip(n, bits):
    return [(i, i ^ bits) for i in range(n)]


tie = lax.optimization_barrier


def place_of():
    return tuple(lax.axis_index(name).astype(jnp.int32) for name in "xzyc")


def chunk_kernel(first_k, count, adds, sizes, b0, b1, b2u, b2d, b3, top, low, *refs):
    before, outs, stage = refs[:adds], refs[adds:-1], refs[-1]
    x, z, y, c = place_of()
    sign = 1 - 2 * (z & 1)
    order = [(z + d * sign) & (NZ - 1) for d in ZORDER[first_k:first_k + count]]
    lam = []
    for zz in order:
        lam += [b0[zz], b1[zz], b2u[zz], b2d[zz], b3[zz]]
    lam = jnp.concatenate(lam, axis=0)
    hi = lam.astype(jnp.bfloat16)
    lo = (lam - hi.astype(jnp.float32)).astype(jnp.bfloat16)
    dot = functools.partial(jnp.dot, preferred_element_type=jnp.float32)
    acc = dot(hi, top[...]) + (dot(lo, top[...]) + dot(hi, low[...]))
    cols = y * 2 * W + lax.broadcasted_iota(jnp.int32, (1, 2 * W), 1)
    first = jnp.zeros((1, 2 * W), jnp.int32)
    last = first
    begin = jnp.int32(0)
    for g in range(GROUPS):
        end = begin + sizes[g]
        inside = (cols >= begin) & (cols < end)
        first = jnp.where(inside, begin, first)
        last = jnp.where(inside, end, last)
        begin = end
    place = c * SUB + (x & 1) * PART + lax.broadcasted_iota(jnp.int32, (PART, 1), 0)
    for k, zz in enumerate(order):
        for rel in range(NY):
            xp = y ^ rel
            row = place + (xp * 1024 + zz * 128)
            at = (k * NY + rel) * PART
            stage[xp] = jnp.where((row >= first) & (row < last), acc[at:at + PART], 0.0)
        for slot in range(3):
            value = stage[0] + stage[3] if slot == 0 else stage[slot]
            for h in range(2):
                piece = value[:, h * W:(h + 1) * W]
                if adds:
                    piece = piece + before[h][first_k + k, slot]
                outs[h][k, slot] = piece


def chunks(sizes, blocks, t2_parts, before, first_k, count):
    whole = pl.BlockSpec(memory_space=pltpu.VMEM)
    return pl.pallas_call(
        functools.partial(chunk_kernel, first_k, count, len(before)),
        out_shape=[jax.ShapeDtypeStruct((count, 3, PART, W), jnp.float32)] * 2,
        in_specs=[pl.BlockSpec(memory_space=pltpu.SMEM)] + [whole] * (7 + len(before)),
        out_specs=[whole, whole],
        scratch_shapes=[pltpu.VMEM((NX, PART, 2 * W), jnp.float32)],
        compiler_params=pltpu.CompilerParams(vmem_limit_bytes=20 * 1024 * 1024),
        cost_estimate=pl.CostEstimate(
            flops=2 * 3 * count * 4 * PART * K * 2 * W,
            bytes_accessed=count * 4 * PART * K * 4 + 4 * K * 2 * W + count * 3 * PART * 2 * W * 4,
            transcendentals=0,
        ),
    )(sizes, *blocks, *t2_parts, *before)


def add_left(full, left):
    n = left.shape[-1]
    return jnp.concatenate([full[..., :n] + left, full[..., n:]], axis=-1)


def add_right(full, right):
    n = full.shape[-1] - right.shape[-1]
    return jnp.concatenate([full[..., :n], full[..., n:] + right], axis=-1)


def step(value, other, axis, n):
    return lax.ppermute(value, axis, even(n)), lax.ppermute(other, axis, odd(n))


def z_first(part):
    half = part[0].shape[-1] // 2
    one, two = tie(step(part[0][..., :half], part[0][..., half:], "z", NZ))
    return tie((add_right(part[1], two), add_left(part[2], one)))


def z_rest(ready, part):
    one, two = step(*ready, "z", NZ)
    for k in (0, 2):
        one, two = tie((one, two))
        one, two = step(*tie((part[k] + two, part[k + 1] + one)), "z", NZ)
    return part[4] + one + two


def split_kernel(masked, count, mine, other, top, low):
    live = lax.broadcasted_iota(jnp.int32, (K, 1), 0) < (count[0] if masked else K)
    c = lax.axis_index("c")

    def put(ref, at):
        value = jnp.where(live, ref[...], 0.0)
        hi = value.astype(jnp.bfloat16)
        top[:, at:at + W] = hi
        low[:, at:at + W] = (value - hi.astype(jnp.float32)).astype(jnp.bfloat16)

    @pl.when(c == 0)
    def _():
        put(mine, 0)
        put(other, W)

    @pl.when(c != 0)
    def _():
        put(other, 0)
        put(mine, W)


def split(masked, count, mine, other):
    whole = pl.BlockSpec(memory_space=pltpu.VMEM)
    return pl.pallas_call(
        functools.partial(split_kernel, masked),
        out_shape=[jax.ShapeDtypeStruct((K, 2 * W), jnp.bfloat16)] * 2,
        in_specs=[pl.BlockSpec(memory_space=pltpu.SMEM), whole, whole],
        out_specs=[whole, whole],
        compiler_params=pltpu.CompilerParams(vmem_limit_bytes=8 * 1024 * 1024),
        cost_estimate=pl.CostEstimate(flops=0, bytes_accessed=16 * K * W, transcendentals=0),
    )(count, mine, other)


def finish_kernel(sizes, mine, other, out):
    x, z, y, c = place_of()
    col = y * 2 * W + c * W + lax.broadcasted_iota(jnp.int32, (1, W), 1)
    first = jnp.zeros((1, W), jnp.int32)
    last = first
    begin = jnp.int32(0)
    for g in range(GROUPS):
        end = begin + sizes[g]
        inside = (col >= begin) & (col < end)
        first = jnp.where(inside, begin, first)
        last = jnp.where(inside, end, last)
        begin = end

    def put(ref, at):
        row = x * 1024 + z * 128 + at + lax.broadcasted_iota(jnp.int32, (SUB, 1), 0)
        out[at:at + SUB] = jnp.where((row >= first) & (row < last), ref[...], 0.0)

    @pl.when(c == 0)
    def _():
        put(mine, 0)
        put(other, SUB)

    @pl.when(c != 0)
    def _():
        put(other, 0)
        put(mine, SUB)


def finish(sizes, mine, other):
    whole = pl.BlockSpec(memory_space=pltpu.VMEM)
    return pl.pallas_call(
        finish_kernel,
        out_shape=jax.ShapeDtypeStruct((2 * SUB, W), jnp.float32),
        in_specs=[pl.BlockSpec(memory_space=pltpu.SMEM), whole, whole],
        out_specs=whole,
        compiler_params=pltpu.CompilerParams(vmem_limit_bytes=4 * 1024 * 1024),
        cost_estimate=pl.CostEstimate(flops=0, bytes_accessed=16 * SUB * W, transcendentals=0),
    )(sizes, mine, other)


def body(t2_amps, lambda_amps, live_pairs, block_sizes):
    x, c = (lax.axis_index(name).astype(jnp.int32) for name in "xc")
    swap = flip(NC, 1)
    places = [c, 1 - c, x & 1, 1 - (x & 1)] + [lax.rem(x ^ d, 3) for d in range(NX)]
    places = [place.astype(jnp.uint32) for place in places]
    lambda_amps, places, low_c, low_p = tie((lambda_amps, places, c == 0, (x & 1) == 0))
    c, not_c, p, not_p, *slots = places
    pick = lambda a, i, axis: lax.dynamic_index_in_dim(a, i, axis, keepdims=False, allow_negative_indices=False)

    def both(at, mine, other, axis):
        return jnp.where(at, jnp.concatenate([mine, other], axis), jnp.concatenate([other, mine], axis))

    lam_rows = lambda_amps.T.reshape(4, NC, SUB, K)
    keep, give = pick(lam_rows, c, 1), pick(lam_rows, not_c, 1)
    live = jnp.arange(K, dtype=jnp.int32)[:, None] < live_pairs[0]
    near = both(low_c, keep, lax.ppermute(give, "c", swap), 0).reshape(NZ, 2, PART, K)
    own = pick(near, p, 1)
    one, two = step(own, own, "y", NY)
    pair = lax.ppermute(pick(near, not_p, 1), "x", flip(NX, 1))

    t2_send, _ = tie((t2_amps, pair))
    t2_soon, _ = tie((t2_amps[:EARLY], own))
    t2_lead = lax.ppermute(jnp.where(live[:EARLY], t2_soon, 0.0), "x", flip(NX, 1))
    t2_par = jnp.concatenate([
        t2_lead,
        lax.ppermute(jnp.where(live[EARLY:], t2_send[EARLY:], 0.0), "x", flip(NX, 1)),
    ])

    half = PART // 2
    fars = two[:, half:], one[:, :half]
    pair, _ = tie((pair, (fars, t2_lead)))
    far_down, far_up = step(*fars, "y", NY)
    blocks = (own, one, far_up, far_down, two)
    one, two = step(pair, pair, "y", NY)
    fars = two[:, half:], one[:, :half]
    fars, _ = tie((fars, (far_down, far_up)))
    t2_late, _ = tie((t2_amps, fars))
    t2_own = split(True, live_pairs, t2_late, lax.ppermute(t2_late, "c", swap))
    first = chunks(block_sizes, blocks, t2_own, (), 0, NZ)
    t2_par, _ = tie((t2_par, fars))
    t2_both, _ = tie(((t2_par, lax.ppermute(t2_par, "c", swap)), first))
    t2_par = split(False, live_pairs, *t2_both)
    far_down, far_up = step(*fars, "y", NY)
    blocks = (pair, one, far_up, far_down, two)
    head = chunks(block_sizes, blocks, t2_par, first, 0, HEAD)
    ready = [z_first(head[h]) for h in range(2)]
    late, ready[0] = tie((block_sizes, ready[0]))
    tail = chunks(late, blocks, t2_par, first, HEAD, NZ - HEAD)
    gots = [z_rest(ready[h], tail[h]) for h in range(2)]
    slot = lambda d: jnp.stack([pick(got, slots[d], 0) for got in gots])
    far = lax.ppermute(slot(2), "x", flip(NX, 2))
    near = lax.ppermute(slot(1), "x", flip(NX, 1))
    wrap = lax.ppermute(slot(3), "x", flip(NX, 3))
    same = slot(0) + far
    (near, wrap), _ = tie(((near, wrap), same))
    done = both(low_p, same, near + wrap, 1)

    mine = jnp.where(low_c, done[0], done[1])
    other = lax.ppermute(jnp.where(low_c, done[1], done[0]), "c", swap)
    return finish(block_sizes, mine, other)


def solution(mesh):
    fine = Mesh(mesh.devices.reshape(NX, NZ, NY, NC), ("x", "z", "y", "c"))
    spec = P(("x", "z"), ("y", "c"))
    return jax.shard_map(
        body,
        mesh=fine,
        in_specs=(spec, spec, P(("x", "z")), P()),
        out_specs=spec,
        check_vma=False,
    )
```

```python
import functools
import jax
import jax.numpy as jnp
from jax import lax
from jax.experimental import pallas as pl
from jax.experimental.pallas import tpu as pltpu
from jax.sharding import Mesh, PartitionSpec as P

NX, NZ, NY, NC = 4, 8, 4, 2
K = 512
W = 512
SUB = 64
PART = 32
ZORDER = (4, 3, -3, 2, -2, 1, -1, 0)
HEAD = 3
GROUPS = 8


def ring(n, away):
    return [(i, (i + away) % n) for i in range(n)]


def even(n):
    return [(i, i ^ 1) for i in range(n)]


def odd(n):
    return [(i, (i + 1) % n if i % 2 else (i - 1) % n) for i in range(n)]


def flip(n, bits):
    return [(i, i ^ bits) for i in range(n)]


tie = lax.optimization_barrier


def place_of():
    return tuple(lax.axis_index(name).astype(jnp.int32) for name in "xzyc")


def chunk_kernel(first_k, count, adds, sizes, b0, b1, b2u, b2d, b3, top, low, *refs):
    before, outs, stage = refs[:adds], refs[adds:-1], refs[-1]
    x, z, y, c = place_of()
    order = [(z + d) & (NZ - 1) for d in ZORDER[first_k:first_k + count]]
    lam = []
    for zz in order:
        lam += [b0[zz], b1[zz], b2u[zz], b2d[zz], b3[zz]]
    lam = jnp.concatenate(lam, axis=0)
    hi = lam.astype(jnp.bfloat16)
    lo = (lam - hi.astype(jnp.float32)).astype(jnp.bfloat16)
    dot = functools.partial(jnp.dot, preferred_element_type=jnp.float32)
    acc = dot(hi, top[...]) + (dot(lo, top[...]) + dot(hi, low[...]))
    cols = y * 2 * W + lax.broadcasted_iota(jnp.int32, (1, 2 * W), 1)
    first = jnp.zeros((1, 2 * W), jnp.int32)
    last = first
    begin = jnp.int32(0)
    for g in range(GROUPS):
        end = begin + sizes[g]
        inside = (cols >= begin) & (cols < end)
        first = jnp.where(inside, begin, first)
        last = jnp.where(inside, end, last)
        begin = end
    place = c * SUB + (x & 1) * PART + lax.broadcasted_iota(jnp.int32, (PART, 1), 0)
    for k, zz in enumerate(order):
        for rel in range(NY):
            xp = y ^ rel
            row = place + (xp * 1024 + zz * 128)
            at = (k * NY + rel) * PART
            stage[xp] = jnp.where((row >= first) & (row < last), acc[at:at + PART], 0.0)
        for slot in range(3):
            value = stage[0] + stage[3] if slot == 0 else stage[slot]
            for h in range(2):
                piece = value[:, h * W:(h + 1) * W]
                if adds:
                    piece = piece + before[h][first_k + k, slot]
                outs[h][k, slot] = piece


def chunks(sizes, blocks, t2_parts, before, first_k, count):
    whole = pl.BlockSpec(memory_space=pltpu.VMEM)
    return pl.pallas_call(
        functools.partial(chunk_kernel, first_k, count, len(before)),
        out_shape=[jax.ShapeDtypeStruct((count, 3, PART, W), jnp.float32)] * 2,
        in_specs=[pl.BlockSpec(memory_space=pltpu.SMEM)] + [whole] * (7 + len(before)),
        out_specs=[whole, whole],
        scratch_shapes=[pltpu.VMEM((NX, PART, 2 * W), jnp.float32)],
        compiler_params=pltpu.CompilerParams(vmem_limit_bytes=20 * 1024 * 1024),
        cost_estimate=pl.CostEstimate(
            flops=2 * 3 * count * 4 * PART * K * 2 * W,
            bytes_accessed=count * 4 * PART * K * 4 + 4 * K * 2 * W + count * 3 * PART * 2 * W * 4,
            transcendentals=0,
        ),
    )(sizes, *blocks, *t2_parts, *before)


def add_left(full, left):
    n = left.shape[-1]
    return jnp.concatenate([full[..., :n] + left, full[..., n:]], axis=-1)


def add_right(full, right):
    n = full.shape[-1] - right.shape[-1]
    return jnp.concatenate([full[..., :n], full[..., n:] + right], axis=-1)


def step(value, other, axis, n):
    return lax.ppermute(value, axis, even(n)), lax.ppermute(other, axis, odd(n))


def turn(up, down):
    return lax.ppermute(up, "z", ring(NZ, 1)), lax.ppermute(down, "z", ring(NZ, -1))


def z_first(part):
    half = part[0].shape[-1] // 2
    one, two = tie(turn(part[0][..., :half], part[0][..., half:]))
    return tie((add_left(part[1], one), add_right(part[2], two)))


def z_rest(ready, part):
    one, two = turn(*ready)
    for k in (0, 2):
        one, two = tie((one, two))
        one, two = turn(*tie((part[k] + one, part[k + 1] + two)))
    return part[4] + one + two


def split_kernel(masked, count, mine, other, top, low):
    live = lax.broadcasted_iota(jnp.int32, (K, 1), 0) < (count[0] if masked else K)
    c = lax.axis_index("c")

    def put(ref, at):
        value = jnp.where(live, ref[...], 0.0)
        hi = value.astype(jnp.bfloat16)
        top[:, at:at + W] = hi
        low[:, at:at + W] = (value - hi.astype(jnp.float32)).astype(jnp.bfloat16)

    @pl.when(c == 0)
    def _():
        put(mine, 0)
        put(other, W)

    @pl.when(c != 0)
    def _():
        put(other, 0)
        put(mine, W)


def split(masked, count, mine, other):
    whole = pl.BlockSpec(memory_space=pltpu.VMEM)
    return pl.pallas_call(
        functools.partial(split_kernel, masked),
        out_shape=[jax.ShapeDtypeStruct((K, 2 * W), jnp.bfloat16)] * 2,
        in_specs=[pl.BlockSpec(memory_space=pltpu.SMEM), whole, whole],
        out_specs=[whole, whole],
        compiler_params=pltpu.CompilerParams(vmem_limit_bytes=8 * 1024 * 1024),
        cost_estimate=pl.CostEstimate(flops=0, bytes_accessed=16 * K * W, transcendentals=0),
    )(count, mine, other)


def finish_kernel(sizes, mine, other, out):
    x, z, y, c = place_of()
    col = y * 2 * W + c * W + lax.broadcasted_iota(jnp.int32, (1, W), 1)
    first = jnp.zeros((1, W), jnp.int32)
    last = first
    begin = jnp.int32(0)
    for g in range(GROUPS):
        end = begin + sizes[g]
        inside = (col >= begin) & (col < end)
        first = jnp.where(inside, begin, first)
        last = jnp.where(inside, end, last)
        begin = end

    def put(ref, at):
        row = x * 1024 + z * 128 + at + lax.broadcasted_iota(jnp.int32, (SUB, 1), 0)
        out[at:at + SUB] = jnp.where((row >= first) & (row < last), ref[...], 0.0)

    @pl.when(c == 0)
    def _():
        put(mine, 0)
        put(other, SUB)

    @pl.when(c != 0)
    def _():
        put(other, 0)
        put(mine, SUB)


def finish(sizes, mine, other):
    whole = pl.BlockSpec(memory_space=pltpu.VMEM)
    return pl.pallas_call(
        finish_kernel,
        out_shape=jax.ShapeDtypeStruct((2 * SUB, W), jnp.float32),
        in_specs=[pl.BlockSpec(memory_space=pltpu.SMEM), whole, whole],
        out_specs=whole,
        compiler_params=pltpu.CompilerParams(vmem_limit_bytes=4 * 1024 * 1024),
        cost_estimate=pl.CostEstimate(flops=0, bytes_accessed=16 * SUB * W, transcendentals=0),
    )(sizes, mine, other)


def body(t2_amps, lambda_amps, live_pairs, block_sizes):
    x, c = (lax.axis_index(name).astype(jnp.int32) for name in "xc")
    swap = flip(NC, 1)
    places = [c, 1 - c, x & 1, 1 - (x & 1)] + [lax.rem(x ^ d, 3) for d in range(NX)]
    places = [place.astype(jnp.uint32) for place in places]
    lambda_amps, places, low_c, low_p = tie((lambda_amps, places, c == 0, (x & 1) == 0))
    c, not_c, p, not_p, *slots = places
    pick = lambda a, i, axis: lax.dynamic_index_in_dim(a, i, axis, keepdims=False, allow_negative_indices=False)

    def both(at, mine, other, axis):
        return jnp.where(at, jnp.concatenate([mine, other], axis), jnp.concatenate([other, mine], axis))

    lam_rows = lambda_amps.T.reshape(4, NC, SUB, K)
    keep, give = pick(lam_rows, c, 1), pick(lam_rows, not_c, 1)
    live = jnp.arange(K, dtype=jnp.int32)[:, None] < live_pairs[0]
    near = both(low_c, keep, lax.ppermute(give, "c", swap), 0).reshape(NZ, 2, PART, K)
    own = pick(near, p, 1)
    one, two = step(own, own, "y", NY)
    pair = lax.ppermute(pick(near, not_p, 1), "x", flip(NX, 1))

    t2_send, _ = tie((t2_amps, pair))
    t2_par = lax.ppermute(jnp.where(live, t2_send, 0.0), "x", flip(NX, 1))

    half = PART // 2
    fars = two[:, half:], one[:, :half]
    pair, _ = tie((pair, fars))
    far_down, far_up = step(*fars, "y", NY)
    blocks = (own, one, far_up, far_down, two)
    one, two = step(pair, pair, "y", NY)
    fars = two[:, half:], one[:, :half]
    fars, _ = tie((fars, (far_down, far_up)))
    t2_late, _ = tie((t2_amps, fars))
    t2_own = split(True, live_pairs, t2_late, lax.ppermute(t2_late, "c", swap))
    first = chunks(block_sizes, blocks, t2_own, (), 0, NZ)
    t2_par, _ = tie((t2_par, fars))
    t2_both, _ = tie(((t2_par, lax.ppermute(t2_par, "c", swap)), first))
    t2_par = split(False, live_pairs, *t2_both)
    far_down, far_up = step(*fars, "y", NY)
    blocks = (pair, one, far_up, far_down, two)
    head = chunks(block_sizes, blocks, t2_par, first, 0, HEAD)
    ready = [z_first(head[h]) for h in range(2)]
    late, ready[0] = tie((block_sizes, ready[0]))
    tail = chunks(late, blocks, t2_par, first, HEAD, NZ - HEAD)
    gots = [z_rest(ready[h], tail[h]) for h in range(2)]
    slot = lambda d: jnp.stack([pick(got, slots[d], 0) for got in gots])
    far = lax.ppermute(slot(2), "x", flip(NX, 2))
    near = lax.ppermute(slot(1), "x", flip(NX, 1))
    wrap = lax.ppermute(slot(3), "x", flip(NX, 3))
    same = slot(0) + far
    (near, wrap), _ = tie(((near, wrap), same))
    done = both(low_p, same, near + wrap, 1)

    mine = jnp.where(low_c, done[0], done[1])
    other = lax.ppermute(jnp.where(low_c, done[1], done[0]), "c", swap)
    return finish(block_sizes, mine, other)


def solution(mesh):
    fine = Mesh(mesh.devices.reshape(NX, NZ, NY, NC), ("x", "z", "y", "c"))
    spec = P(("x", "z"), ("y", "c"))
    return jax.shard_map(
        body,
        mesh=fine,
        in_specs=(spec, spec, P(("x", "z")), P()),
        out_specs=spec,
        check_vma=False,
    )
```
